32 devices in a mesh: front: 8 (over y, x, core), enc: 4 (over z).
Axes of the slice: x: 2, y: 2, z: 4, core: 2. Of those that a mesh axis runs over, the one named last changes fastest.
Arguments:
- spectra: bfloat16 [1024, 56, 80], P('front'), may hold values from -6 to 6
- sub_weight: bfloat16 [640, 1024], P(None, 'enc'), may hold values from -0.25 to 0.25
- sub_bias: bfloat16 [1024], P('enc'), may hold values from -4 to 4
- key_cache: bfloat16 [1024, 70, 1024], P('front', None, 'enc'), may hold values from -1000 to 1000
- value_cache: bfloat16 [1024, 70, 1024], P('front', None, 'enc'), may hold values from -6 to 6
- conv_cache: bfloat16 [1024, 8, 1024], P('front', None, 'enc'), may hold values from -6 to 6
- new_slot: int32 [1024], P('front'), may hold values from 0 to 1023, as said below
- old_slot: int32 [1024], P('front'), may hold values from 0 to 1023, as said below
- valid_new: int32 [1024], P('front'), may hold values from 1 to 7
- cache_fill: int32 [1024], P('front'), may hold values from 0 to 70
- ln1_gain: float32 [1024], replicated, may hold values from 0.5 to 1.5
- w_query: bfloat16 [1024, 1024], P(None, 'enc'), may hold values from -0.1875 to 0.1875
- w_key: bfloat16 [1024, 1024], P(None, 'enc'), may hold values from -0.1875 to 0.1875
- w_value: bfloat16 [1024, 1024], P(None, 'enc'), may hold values from -0.1875 to 0.1875
- w_attn_out: bfloat16 [1024, 1024], P('enc'), may hold values from -0.1875 to 0.1875
- ln2_gain: float32 [1024], replicated, may hold values from 0.5 to 1.5
- w_glu_value: bfloat16 [1024, 1024], P(None, 'enc'), may hold values from -0.1875 to 0.1875
- w_glu_gate: bfloat16 [1024, 1024], P(None, 'enc'), may hold values from -0.1875 to 0.1875
- depth_kernel: float32 [9, 1024], P(None, 'enc'), may hold values from -2 to 2
- norm_scale: float32 [1024], P('enc'), may hold values from 0.1 to 1.9
- norm_shift: float32 [1024], P('enc'), may hold values from -3 to 3
- w_conv_out: bfloat16 [1024, 1024], P('enc'), may hold values from -0.1875 to 0.1875
Outputs:
- encoded: bfloat16 [1024, 7, 1024], P('front', None, 'enc')
- key_out: bfloat16 [1024, 70, 1024], P('front', None, 'enc')
- value_out: bfloat16 [1024, 70, 1024], P('front', None, 'enc')
- conv_out: bfloat16 [1024, 8, 1024], P('front', None, 'enc')
The draws below stay inside these ranges and needn't reach their ends.
Inputs may be any that keep to these rules, and one draw needn't show every extreme that they name: `new_slot`: A permutation of the stream slots. Device f of front holds old slots and new slots f * 128 to (f + 1) * 128 - 1; a stream that stays on its device keeps its slot; each device hands at most 2 streams to any other device, to at most 4 other devices, and receives as many streams as it hands away. `old_slot`: the inverse permutation of new_slot.
All inputs are finite; a program needn't handle non-finite values.
Results may differ from the reference program's by a relative error of at most 0.0095.
Values may be sent and summed in bfloat16 or wider, within the bound.
A program may use at most 128 MiB of HBM per device.

```python
import math
import jax
import jax.numpy as jnp
from jax import lax

D = 1024
HEADS = 8
MELS = 80
KERNEL = 9
SUB = 8
FRAMES = 7
CACHE = 70
CAP = 2
S_DEV = 128
HEAD = 128
MEL_FRAMES = 56
CONV_CACHE = 8
STREAMS = 1024
N_ENC = 4


def slot_tables(key):
    base_key = jax.random.fold_in(key, 1234)
    owners = STREAMS // S_DEV
    rounds = owners // 2
    key_relabel, key_shift, key_count, key_order = jax.random.split(base_key, 4)
    relabel = jax.random.permutation(key_relabel, owners)
    inverse = jnp.argsort(relabel)
    shifts = 1 + jax.random.permutation(key_shift, owners - 1)[:rounds]
    counts = jax.random.randint(key_count, (rounds,), 1, CAP + 1).at[0].set(CAP)
    round_ends = jnp.cumsum(counts)
    orders = jax.vmap(lambda sub_key: jax.random.permutation(sub_key, S_DEV))(jax.random.split(key_order, owners))
    place_index = jnp.arange(S_DEV, dtype=jnp.int32)
    round_of = jnp.sum((place_index[:, None] >= round_ends[None, :]).astype(jnp.int32), axis=1)
    moving = place_index < round_ends[-1]
    round_clip = jnp.minimum(round_of, rounds - 1)
    device_index = jnp.arange(owners, dtype=jnp.int32)
    target = inverse[(relabel[:, None] + shifts[round_clip][None, :]) % owners]
    target = jnp.where(moving[None, :], target, device_index[:, None])
    dest_local = orders[target, jnp.broadcast_to(place_index[None, :], target.shape)]
    dest_slot = target * S_DEV + dest_local
    source_slot = device_index[:, None] * S_DEV + orders
    new_table = jnp.zeros((STREAMS,), jnp.int32).at[source_slot.reshape(-1)].set(dest_slot.reshape(-1).astype(jnp.int32))
    old_table = jnp.zeros((STREAMS,), jnp.int32).at[new_table].set(jnp.arange(STREAMS, dtype=jnp.int32))
    return (new_table, old_table)


def draw_new_slot(key, part):
    return slot_tables(key)[0]


def draw_old_slot(key, part):
    return slot_tables(key)[1]


def draw_key_cache(key, part):
    key_base = jax.random.fold_in(jax.random.fold_in(key, 99), 0)
    drawn = jnp.clip(jax.random.normal(key_base, (STREAMS, CACHE, D), jnp.float32), -6.0, 6.0)
    return drawn.astype(jnp.bfloat16)


def touch_ends(entries, stream_key, smallest, top_value):
    longest = entries.shape.index(max(entries.shape))
    spots = []
    for shift in (0, 1):
        where = [jax.random.randint(jax.random.fold_in(stream_key, axis), (), 0, length) for axis, length in enumerate(entries.shape)]
        where[longest] = (where[longest] + shift) % entries.shape[longest]
        spots.append(tuple(where))
    return entries.at[spots[0]].set(smallest).at[spots[1]].set(top_value)


def level_of(own_key, dims, shards, least, largest):
    def one(axis_at, shards_of):
        heights = jax.random.uniform(jax.random.fold_in(jax.random.fold_in(own_key, 6), axis_at), (shards_of,), jnp.float32, least / len(shards), largest / len(shards))
        return jnp.repeat(jnp.exp(heights), dims[axis_at] // shards_of).reshape((-1,) + (1,) * (len(dims) - axis_at - 1))

    gain = one(*shards[0])
    for cut in shards[1:]:
        gain = gain * one(*cut)
    return gain


def bell_draw(own_key, extent, deviation, limit, cuts=(), kind=jnp.bfloat16):
    level = level_of(own_key, extent, cuts, -0.22, 0.18) if cuts else 1.0
    entries = jax.random.normal(own_key, extent, jnp.float32) * deviation * level
    return jnp.minimum(jnp.maximum(entries, -limit), limit).astype(kind)


def setup_inputs(seed: int = 0) -> dict:
    arg_keys = jax.random.split(jax.random.key(seed), 23)
    return {
        "spectra": bell_draw(arg_keys[0], (STREAMS, MEL_FRAMES, MELS), 1.0, 6.0, ((0, 8),)),
        "sub_weight": bell_draw(arg_keys[1], (SUB * MELS, D), (SUB * MELS) ** -0.5, 0.25, ((1, 4),)),
        "sub_bias": bell_draw(arg_keys[2], (D,), 1.0, 4.0, ((0, 4),)),
        "key_cache": draw_key_cache(jax.random.fold_in(arg_keys[22], 71), 0),
        "value_cache": bell_draw(arg_keys[4], (STREAMS, CACHE, D), 1.0, 6.0, ((0, 8), (2, 4))),
        "conv_cache": bell_draw(arg_keys[5], (STREAMS, CONV_CACHE, D), 1.0, 6.0, ((0, 8), (2, 4))),
        "new_slot": draw_new_slot(jax.random.fold_in(arg_keys[22], 71), 0),
        "old_slot": draw_old_slot(jax.random.fold_in(arg_keys[22], 71), 0),
        "valid_new": touch_ends(jax.random.randint(arg_keys[8], (STREAMS,), 1, FRAMES + 1), jax.random.fold_in(arg_keys[8], 1), 1, FRAMES).astype(jnp.int32),
        "cache_fill": touch_ends(jax.random.randint(arg_keys[9], (STREAMS,), 0, CACHE + 1), jax.random.fold_in(arg_keys[9], 1), 0, CACHE).astype(jnp.int32),
        "ln1_gain": jnp.clip(1.0 + 0.1 * jax.random.normal(arg_keys[10], (D,), jnp.float32), 0.5, 1.5),
        "w_query": bell_draw(arg_keys[11], (D, D), D ** -0.5, 0.1875, ((1, 4),)),
        "w_key": bell_draw(arg_keys[12], (D, D), D ** -0.5, 0.1875, ((1, 4),)),
        "w_value": bell_draw(arg_keys[13], (D, D), D ** -0.5, 0.1875, ((1, 4),)),
        "w_attn_out": bell_draw(arg_keys[14], (D, D), D ** -0.5, 0.1875, ((0, 4),)),
        "ln2_gain": jnp.clip(1.0 + 0.1 * jax.random.normal(arg_keys[15], (D,), jnp.float32), 0.5, 1.5),
        "w_glu_value": bell_draw(arg_keys[16], (D, D), D ** -0.5, 0.1875, ((1, 4),)),
        "w_glu_gate": bell_draw(arg_keys[17], (D, D), D ** -0.5, 0.1875, ((1, 4),)),
        "depth_kernel": bell_draw(arg_keys[18], (KERNEL, D), KERNEL ** -0.5, 2.0, ((1, 4),), jnp.float32),
        "norm_scale": jnp.clip(1.0 + 0.18 * jax.random.normal(arg_keys[19], (D,), jnp.float32), 0.1, 1.9),
        "norm_shift": bell_draw(arg_keys[20], (D,), 0.5, 3.0, ((0, 4),), jnp.float32),
        "w_conv_out": bell_draw(arg_keys[21], (D, D), D ** -0.5, 0.1875, ((0, 4),)),
    }


masked_score = -1e+30

def layer_norm(values_in, scale_gain):
    average = lax.optimization_barrier(jnp.mean(values_in, axis=-1, keepdims=True))
    centered = values_in - average
    spread = lax.optimization_barrier(jnp.mean(centered * centered, axis=-1, keepdims=True))
    return centered * lax.rsqrt(spread + 1e-05) * scale_gain

def grouped_sum(operand, matrix):
    slice_width = operand.shape[1] // N_ENC
    summed = jnp.zeros((operand.shape[0], matrix.shape[1]), jnp.float32)
    for member in range(N_ENC):
        portion = jnp.dot(operand[:, member * slice_width:(member + 1) * slice_width], matrix[member * slice_width:(member + 1) * slice_width], preferred_element_type=jnp.float32)
        rounded = lax.optimization_barrier(portion.astype(jnp.bfloat16))
        summed = summed + rounded.astype(jnp.float32)
    return summed

def trim_rows(block_all, offsets, length):
    return jax.vmap(lambda block_rows, offset_rows: lax.dynamic_slice_in_dim(block_rows, offset_rows, length, 0))(block_all, offsets)

def reference(spectra, sub_weight, sub_bias, key_cache, value_cache, conv_cache, new_slot, old_slot, valid_new, cache_fill, ln1_gain, w_query, w_key, w_value, w_attn_out, ln2_gain, w_glu_value, w_glu_gate, depth_kernel, norm_scale, norm_shift, w_conv_out):
    streams = spectra.shape[0]
    stacked = spectra.reshape(streams * FRAMES, SUB * MELS)
    subsampled = (jnp.dot(stacked, sub_weight, preferred_element_type=jnp.float32) + sub_bias.astype(jnp.float32)).astype(jnp.bfloat16)
    subsampled = subsampled.reshape(streams, FRAMES, D)
    inputs = jnp.take(subsampled, old_slot, axis=0)
    keys_old = jnp.zeros_like(key_cache).at[new_slot].set(key_cache)
    values_old = jnp.zeros_like(value_cache).at[new_slot].set(value_cache)
    conv_old = jnp.zeros_like(conv_cache).at[new_slot].set(conv_cache)
    flat_in = inputs.reshape(streams * FRAMES, D)
    normed = layer_norm(flat_in.astype(jnp.float32), ln1_gain).astype(jnp.bfloat16)
    queries = jnp.dot(normed, w_query, preferred_element_type=jnp.float32).astype(jnp.bfloat16).reshape(streams, FRAMES, HEADS, HEAD)
    key_new = jnp.dot(normed, w_key, preferred_element_type=jnp.float32).astype(jnp.bfloat16).reshape(streams, FRAMES, HEADS, HEAD)
    value_new = jnp.dot(normed, w_value, preferred_element_type=jnp.float32).astype(jnp.bfloat16).reshape(streams, FRAMES, HEADS, HEAD)
    keys_all = jnp.concatenate([keys_old.reshape(streams, CACHE, HEADS, HEAD), key_new], axis=1)
    values_all = jnp.concatenate([values_old.reshape(streams, CACHE, HEADS, HEAD), value_new], axis=1)
    scores = jnp.einsum('sthd,sjhd->shtj', queries.astype(jnp.float32), keys_all.astype(jnp.float32)) / math.sqrt(HEAD)
    position = jnp.arange(CACHE + FRAMES, dtype=jnp.int32)[None, :]
    cache_ok = (position < CACHE) & (position >= CACHE - cache_fill[:, None])
    new_ok = (position >= CACHE) & (position - CACHE < valid_new[:, None])
    allowed = (cache_ok | new_ok)[:, None, None, :]
    scores = jnp.where(allowed, scores, masked_score)
    row_peak = lax.optimization_barrier(jnp.max(scores, axis=-1, keepdims=True))
    exponent = jnp.where(allowed, jnp.exp(scores - row_peak), 0.0)
    weights = (exponent / lax.optimization_barrier(jnp.sum(exponent, axis=-1, keepdims=True))).astype(jnp.bfloat16)
    context = jnp.einsum('shtj,sjhd->sthd', weights.astype(jnp.float32), values_all.astype(jnp.float32)).astype(jnp.bfloat16)
    context = context.reshape(streams * FRAMES, D)
    attended = grouped_sum(context, w_attn_out)
    middle = (flat_in.astype(jnp.float32) + attended).astype(jnp.bfloat16)
    normed_second = layer_norm(middle.astype(jnp.float32), ln2_gain).astype(jnp.bfloat16)
    glu_value = jnp.dot(normed_second, w_glu_value, preferred_element_type=jnp.float32)
    glu_gate = jnp.dot(normed_second, w_glu_gate, preferred_element_type=jnp.float32)
    gated = (glu_value * jax.nn.sigmoid(glu_gate)).astype(jnp.bfloat16).reshape(streams, FRAMES, D)
    conv_in = jnp.concatenate([conv_old, gated], axis=1)
    depthwise = jnp.zeros((streams, FRAMES, D), jnp.float32)
    for kernel_tap in range(KERNEL):
        depthwise = depthwise + depth_kernel[kernel_tap] * conv_in[:, kernel_tap:kernel_tap + FRAMES].astype(jnp.float32)
    shaped = depthwise * norm_scale + norm_shift
    activated = (shaped * jax.nn.sigmoid(shaped)).astype(jnp.bfloat16).reshape(streams * FRAMES, D)
    conv_term = grouped_sum(activated, w_conv_out)
    frame_ok = (jnp.arange(FRAMES, dtype=jnp.int32)[None, :] < valid_new[:, None]).astype(jnp.float32)
    encoded = ((middle.astype(jnp.float32) + conv_term).reshape(streams, FRAMES, D) * frame_ok[:, :, None]).astype(jnp.bfloat16)
    key_out = trim_rows(keys_all.reshape(streams, CACHE + FRAMES, D), valid_new, CACHE)
    value_out = trim_rows(values_all.reshape(streams, CACHE + FRAMES, D), valid_new, CACHE)
    conv_out = trim_rows(conv_in, valid_new, CONV_CACHE)
    return (encoded, key_out, value_out, conv_out)
```

```python
import functools
import math

import jax
import jax.numpy as jnp
from jax import lax
from jax.experimental import pallas as pl
from jax.experimental.pallas import tpu as pltpu
from jax.sharding import PartitionSpec as P

KERNEL = 9
SUB = 8
FRAMES = 7
CACHE = 70
TOTAL = CACHE + FRAMES
CAP = 2
HEAD = 128
CONV_CACHE = 8
GROUP = 16
VMEM_LIMIT = 56 * 1024 * 1024

masked_score = -1e30
BF = jnp.bfloat16
F32 = jnp.float32


def mm(a, b):
    return jnp.dot(a, b, preferred_element_type=F32)


def layer_norm(values_in, gain):
    average = jnp.mean(values_in, axis=-1, keepdims=True)
    centered = values_in - average
    spread = jnp.mean(centered * centered, axis=-1, keepdims=True)
    return centered * lax.rsqrt(spread + 1e-05) * gain


def send_slots(new_slot, own_index, peer_count, stream_count):
    target = new_slot // stream_count
    leaving = target != own_index
    index = jnp.arange(stream_count, dtype=jnp.int32)
    earlier = (target[None, :] == target[:, None]) & (index[None, :] < index[:, None])
    position = jnp.sum(earlier.astype(jnp.int32), axis=1)
    bucket = jnp.where(leaving, target * CAP + position, peer_count * CAP)
    return bucket[None, :] == jnp.arange(peer_count * CAP, dtype=jnp.int32)[:, None]


def arrival_slots(old_slot, own_index, slots):
    stream_count = old_slot.shape[0]
    source = old_slot // stream_count
    staying = source == own_index
    earlier = (source[None, :] == source[:, None]) & (old_slot[None, :] < old_slot[:, None])
    position = jnp.sum(earlier.astype(jnp.int32), axis=1)
    arrival = jnp.where(staying, slots, source * CAP + position)
    return arrival, staying


def shift_rows(block, masks):
    for mask, step in zip(masks, (1, 2, 4)):
        block = jnp.where(mask[None], block[step:], block[:-step])
    return block


def project_kernel(x_ref, sw_ref, sb_ref, gain_ref, wq_ref, wk_ref, wv_ref, in_ref, q_ref, k_ref, v_ref):
    x = x_ref[0]
    parts = []
    for g in range(sw_ref.shape[0]):
        part = lax.dot_general(x, sw_ref[g], (((0,), (0,)), ((), ())), preferred_element_type=F32)
        parts.append(part)
    inputs = (jnp.concatenate(parts, axis=1) + sb_ref[...]).astype(BF)
    in_ref[0] = inputs
    normed = layer_norm(inputs.astype(F32), gain_ref[...]).astype(BF)
    q_ref[0] = mm(normed, wq_ref[...]).astype(BF)
    k_ref[0] = mm(normed, wk_ref[...]).astype(BF)
    v_ref[0] = mm(normed, wv_ref[...]).astype(BF)


def project(x, sw, sb, gain, wq, wk, wv):
    frames, depth, streams = x.shape
    width = wq.shape[0]
    local = wq.shape[1]
    whole = lambda shape: pl.BlockSpec(shape, lambda t: (0,) * len(shape))
    row = lambda w: pl.BlockSpec((1, streams, w), lambda t: (t, 0, 0))
    return pl.pallas_call(
        project_kernel,
        grid=(frames,),
        in_specs=[
            pl.BlockSpec((1, depth, streams), lambda t: (t, 0, 0)),
            whole(sw.shape),
            whole(sb.shape),
            whole(gain.shape),
            whole(wq.shape),
            whole(wk.shape),
            whole(wv.shape),
        ],
        out_specs=[row(width), row(local), row(local), row(local)],
        out_shape=[jax.ShapeDtypeStruct((frames, streams, width), BF)]
        + [jax.ShapeDtypeStruct((frames, streams, local), BF)] * 3,
        compiler_params=pltpu.CompilerParams(vmem_limit_bytes=VMEM_LIMIT),
        name="project",
    )(x, sw, sb, gain, wq, wk, wv)


def attend_kernel(
    has_ref, q_ref, kn_ref, vn_ref, kc_ref, vc_ref, kr_ref, vr_ref, pick_ref, bits_ref, stay_ref,
    colbias_ref, match_ref, ctx_ref, ko_ref, vo_ref, kall, vall,
):
    group = pl.program_id(0)
    local = q_ref.shape[2]
    slots = kr_ref.shape[1]
    span = pick_ref.shape[2] // slots
    kall[0:CACHE] = kc_ref[...]
    vall[0:CACHE] = vc_ref[...]

    @pl.when(has_ref[group] > 0)
    def _():
        stay = (stay_ref[...] > 0.5)[None]
        for first in range(0, CACHE, span):
            count = min(span, CACHE - first)
            pick = pick_ref[0, : count * GROUP, : count * slots]
            for rec, dest in ((kr_ref, kall), (vr_ref, vall)):
                rows = rec[first : first + count].reshape(count * slots, local)
                fetched = mm(pick, rows).astype(BF).reshape(count, GROUP, local)
                dest[first : first + count] = jnp.where(stay, dest[first : first + count], fetched)

    kall[CACHE:TOTAL] = kn_ref[...]
    vall[CACHE:TOTAL] = vn_ref[...]
    bias = match_ref[...] + colbias_ref[0]
    for h in range(local // HEAD):
        lanes = slice(h * HEAD, (h + 1) * HEAD)
        qh = q_ref[:, :, lanes].reshape(FRAMES * GROUP, HEAD)
        kh = kall[:, :, lanes].reshape(TOTAL * GROUP, HEAD)
        vh = vall[:, :, lanes].reshape(TOTAL * GROUP, HEAD)
        scores = lax.dot_general(qh, kh, (((1,), (1,)), ((), ())), preferred_element_type=F32)
        scores = scores * (1.0 / math.sqrt(HEAD)) + bias
        peak = jnp.max(scores, axis=-1, keepdims=True)
        expo = jnp.exp(scores - peak)
        weights = (expo * (1.0 / jnp.sum(expo, axis=-1, keepdims=True))).astype(BF)
        ctx_ref[:, :, lanes] = mm(weights, vh).astype(BF).reshape(FRAMES, GROUP, HEAD)
    masks = [bits_ref[b] > 0.5 for b in range(3)]
    step = 10
    for src, dst in ((kall, ko_ref), (vall, vo_ref)):
        for first in range(0, CACHE, step):
            dst[first : first + step] = shift_rows(src[first : first + step + FRAMES], masks)


def attend(has, q, kn, vn, kc, vc, kr, vr, pick, bits, stay, colbias, match):
    streams, local = q.shape[1:]
    groups = streams // GROUP
    slots = kr.shape[1]
    block = lambda n: pl.BlockSpec((n, GROUP, local), lambda g, *_: (0, g, 0))
    whole = lambda shape: pl.BlockSpec(shape, lambda g, *_: (0,) * len(shape))
    return pl.pallas_call(
        attend_kernel,
        grid_spec=pltpu.PrefetchScalarGridSpec(
            num_scalar_prefetch=1,
            grid=(groups,),
            in_specs=[
                block(FRAMES), block(FRAMES), block(FRAMES), block(CACHE), block(CACHE),
                whole(kr.shape), whole(vr.shape),
                pl.BlockSpec((1,) + pick.shape[1:], lambda g, *_: (g, 0, 0)),
                block(3),
                pl.BlockSpec((GROUP, local), lambda g, *_: (g, 0)),
                pl.BlockSpec((1, 1, TOTAL * GROUP), lambda g, *_: (g, 0, 0)),
                whole(match.shape),
            ],
            out_specs=[block(FRAMES), block(CACHE), block(CACHE)],
            scratch_shapes=[pltpu.VMEM((TOTAL, GROUP, local), BF)] * 2,
        ),
        out_shape=[
            jax.ShapeDtypeStruct((FRAMES, streams, local), BF),
            jax.ShapeDtypeStruct((CACHE, streams, local), BF),
            jax.ShapeDtypeStruct((CACHE, streams, local), BF),
        ],
        compiler_params=pltpu.CompilerParams(vmem_limit_bytes=VMEM_LIMIT),
        cost_estimate=pl.CostEstimate(flops=1200000000, bytes_accessed=20000000, transcendentals=2500000),
        name="attend",
    )(has, q, kn, vn, kc, vc, kr, vr, pick, bits, stay, colbias, match)


def convolve_kernel(
    ctx_ref, in_ref, wo_ref, gain_ref, wv_ref, wg_ref, conv_ref, bits_ref, dk_ref, scale_ref, bias_ref,
    mid_ref, act_ref, co_ref, conv_all,
):
    parts, frames, streams, local = ctx_ref.shape
    width = in_ref.shape[2]
    rows = frames * streams
    attended = jnp.zeros((rows, width), F32)
    for g in range(parts):
        share = mm(ctx_ref[g].reshape(rows, local), wo_ref[g * local : (g + 1) * local])
        attended = attended + share.astype(BF).astype(F32)
    middle = (in_ref[...].reshape(rows, width).astype(F32) + attended).astype(BF)
    mid_ref[...] = middle.reshape(frames, streams, width)
    normed = layer_norm(middle.astype(F32), gain_ref[...]).astype(BF)
    gated = (mm(normed, wv_ref[...]) * jax.nn.sigmoid(mm(normed, wg_ref[...]))).astype(BF)
    conv_all[0:CONV_CACHE] = conv_ref[...]
    conv_all[CONV_CACHE:] = gated.reshape(frames, streams, local)
    taps = [dk_ref[k : k + 1, :] for k in range(KERNEL)]
    for t in range(frames):
        total = jnp.zeros((streams, local), F32)
        for k in range(KERNEL):
            total = total + taps[k] * conv_all[t + k].astype(F32)
        shaped = total * scale_ref[...] + bias_ref[...]
        act_ref[t] = (shaped * jax.nn.sigmoid(shaped)).astype(BF)
    co_ref[...] = shift_rows(conv_all[...], [bits_ref[b] > 0.5 for b in range(3)])


def convolve(ctx, inputs, wo, gain, wv, wg, conv, bits, dk, scale, bias):
    parts, frames, streams, local = ctx.shape
    width = inputs.shape[2]
    size = min(64, streams)
    whole = lambda shape: pl.BlockSpec(shape, lambda g: (0,) * len(shape))
    block = lambda n, w: pl.BlockSpec((n, size, w), lambda g: (0, g, 0))
    return pl.pallas_call(
        convolve_kernel,
        grid=(streams // size,),
        in_specs=[
            pl.BlockSpec((parts, frames, size, local), lambda g: (0, 0, g, 0)),
            block(frames, width),
            whole(wo.shape), whole(gain.shape), whole(wv.shape), whole(wg.shape),
            block(CONV_CACHE, local), block(3, local),
            whole(dk.shape), whole(scale.shape), whole(bias.shape),
        ],
        out_specs=[block(frames, width), block(frames, local), block(CONV_CACHE, local)],
        out_shape=[
            jax.ShapeDtypeStruct((frames, streams, width), BF),
            jax.ShapeDtypeStruct((frames, streams, local), BF),
            jax.ShapeDtypeStruct((CONV_CACHE, streams, local), BF),
        ],
        scratch_shapes=[pltpu.VMEM((CONV_CACHE + frames, size, local), BF)],
        compiler_params=pltpu.CompilerParams(vmem_limit_bytes=VMEM_LIMIT),
        name="convolve",
    )(ctx, inputs, wo, gain, wv, wg, conv, bits, dk, scale, bias)


def finish_kernel(me_ref, act_ref, wc_ref, mid_ref, valid_ref, out_ref):
    parts, frames, streams, local = act_ref.shape
    rows = frames * streams
    total = jnp.zeros((rows, local), F32)
    for g in range(parts):
        share = mm(act_ref[g].reshape(rows, local), wc_ref[g * local : (g + 1) * local])
        total = total + share.astype(BF).astype(F32)
    total = total + mid_ref[...].reshape(rows, local).astype(F32)
    total = total.reshape(frames, streams, local)
    for t in range(frames):
        out_ref[t] = jnp.where(valid_ref[...] > t + 0.5, total[t], 0.0).astype(BF)


def finish(me, act, wc, middle, valid_wide):
    parts, frames, streams, local = act.shape
    size = min(64, streams)
    return pl.pallas_call(
        finish_kernel,
        grid_spec=pltpu.PrefetchScalarGridSpec(
            num_scalar_prefetch=1,
            grid=(streams // size,),
            in_specs=[
                pl.BlockSpec((parts, frames, size, local), lambda g, m: (0, 0, g, 0)),
                pl.BlockSpec(wc.shape, lambda g, m: (0, 0)),
                pl.BlockSpec((frames, size, local), lambda g, m: (0, g, m[0])),
                pl.BlockSpec((size, local), lambda g, m: (g, 0)),
            ],
            out_specs=pl.BlockSpec((frames, size, local), lambda g, m: (0, g, 0)),
        ),
        out_shape=jax.ShapeDtypeStruct((frames, streams, local), BF),
        compiler_params=pltpu.CompilerParams(vmem_limit_bytes=VMEM_LIMIT),
        name="finish",
    )(me, act, wc, middle, valid_wide)


def on_device(
    spectra,
    sub_weight,
    sub_bias,
    key_cache,
    value_cache,
    conv_cache,
    new_slot,
    old_slot,
    valid_new,
    cache_fill,
    ln1_gain,
    w_query,
    w_key,
    w_value,
    w_attn_out,
    ln2_gain,
    w_glu_value,
    w_glu_gate,
    depth_kernel,
    norm_scale,
    norm_shift,
    w_conv_out,
):
    peer_count = lax.axis_size("front")
    own_index = lax.axis_index("front")
    member = lax.axis_index("enc")
    streams = spectra.shape[0]
    local = w_query.shape[1]
    slots = peer_count * CAP
    mels = spectra.shape[2]

    sub_full = lax.all_gather(sub_weight, "enc")
    bias_full = lax.all_gather(sub_bias, "enc", tiled=True).astype(F32)[None]
    attn_full = lax.all_gather(w_attn_out, "enc", tiled=True)
    conv_cols = lax.all_to_all(w_conv_out, "enc", split_axis=1, concat_axis=0, tiled=True)

    leaving = send_slots(new_slot, own_index, peer_count, streams).astype(BF)
    arrival, staying = arrival_slots(old_slot, own_index, slots)
    arriving = (arrival[:, None] == jnp.arange(slots, dtype=jnp.int32)[None, :]).astype(BF)

    x = spectra.transpose(1, 2, 0).reshape(FRAMES * SUB * mels, streams)
    x_send = lax.dot_general(leaving, x, (((1,), (1,)), ((), ())), preferred_element_type=F32).astype(BF)
    x_recv = lax.all_to_all(x_send, "front", split_axis=0, concat_axis=0, tiled=True)
    x_moved = lax.dot_general(x_recv, arriving, (((0,), (1,)), ((), ())), preferred_element_type=F32).astype(BF)
    x_new = jnp.where(staying[None, :], x, x_moved).reshape(FRAMES, SUB * mels, streams)

    keys = key_cache.transpose(1, 0, 2)
    values = value_cache.transpose(1, 0, 2)
    conv = conv_cache.transpose(1, 0, 2)
    choose = lambda a: jnp.einsum("rs,jsc->rjc", leaving, a, preferred_element_type=F32).astype(BF)
    bundle = jnp.concatenate([choose(keys), choose(values), choose(conv)], axis=1)
    recv = lax.all_to_all(bundle, "front", split_axis=0, concat_axis=0, tiled=True).transpose(1, 0, 2)
    keys_recv, values_recv = recv[:CACHE], recv[CACHE : 2 * CACHE]
    conv_moved = jnp.einsum(
        "sr,jrc->jsc", arriving, recv[2 * CACHE :], preferred_element_type=F32
    ).astype(BF)
    conv_old = jnp.where(staying[None, :, None], conv, conv_moved)

    groups = streams // GROUP
    span = max(1, 256 // slots)
    pick = jnp.einsum(
        "ab,gnr->ganbr", jnp.eye(span, dtype=BF), arriving.reshape(groups, GROUP, slots)
    ).reshape(groups, span * GROUP, span * slots)
    has = jnp.sum((~staying).astype(jnp.int32).reshape(groups, GROUP), axis=1)
    valid_wide = jnp.broadcast_to(valid_new.astype(F32)[:, None], (streams, local))
    bits = jnp.stack([(valid_new >> b) & 1 for b in range(3)]).astype(BF)
    bits = jnp.broadcast_to(bits[:, :, None], (3, streams, local))
    stay_wide = jnp.broadcast_to(staying.astype(BF)[:, None], (streams, local))
    position = jnp.arange(TOTAL, dtype=jnp.int32)[:, None]
    cache_ok = (position < CACHE) & (position >= CACHE - cache_fill[None, :])
    new_ok = (position >= CACHE) & (position - CACHE < valid_new[None, :])
    colbias = jnp.where(cache_ok | new_ok, 0.0, masked_score).astype(F32)
    colbias = colbias.reshape(TOTAL, groups, GROUP).transpose(1, 0, 2).reshape(groups, 1, TOTAL * GROUP)
    row_of = jnp.arange(FRAMES * GROUP, dtype=jnp.int32) % GROUP
    col_of = jnp.arange(TOTAL * GROUP, dtype=jnp.int32) % GROUP
    match = jnp.where(row_of[:, None] == col_of[None, :], 0.0, masked_score).astype(F32)

    inputs, queries, key_new, value_new = project(
        x_new, sub_full, bias_full, ln1_gain[None], w_query, w_key, w_value
    )
    context, key_out, value_out = attend(
        has, queries, key_new, value_new, keys, values, keys_recv, values_recv, pick, bits, stay_wide,
        colbias, match,
    )
    context_full = lax.all_gather(context, "enc")
    middle, activated, conv_out = convolve(
        context_full, inputs, attn_full, ln2_gain[None], w_glu_value, w_glu_gate, conv_old, bits,
        depth_kernel, norm_scale[None], norm_shift[None],
    )
    act_full = lax.all_gather(activated, "enc")
    encoded = finish(member.astype(jnp.int32)[None], act_full, conv_cols, middle, valid_wide)
    back = lambda a: a.transpose(1, 0, 2)
    return back(encoded), back(key_out), back(value_out), back(conv_out)


def solution(mesh):
    in_specs = (
        P("front", None, None),
        P(None, "enc"),
        P("enc"),
        P("front", None, "enc"),
        P("front", None, "enc"),
        P("front", None, "enc"),
        P("front"),
        P("front"),
        P("front"),
        P("front"),
        P(),
        P(None, "enc"),
        P(None, "enc"),
        P(None, "enc"),
        P("enc", None),
        P(),
        P(None, "enc"),
        P(None, "enc"),
        P(None, "enc"),
        P("enc"),
        P("enc"),
        P("enc", None),
    )
    out_specs = (P("front", None, "enc"),) * 4
    return jax.shard_map(
        on_device, mesh=mesh, in_specs=in_specs, out_specs=out_specs, check_vma=False
    )
```

```python
import functools
import math

import jax
import jax.numpy as jnp
from jax import lax
from jax.experimental import pallas as pl
from jax.experimental.pallas import tpu as pltpu
from jax.sharding import PartitionSpec as P

KERNEL = 9
SUB = 8
FRAMES = 7
CACHE = 70
TOTAL = CACHE + FRAMES
CAP = 2
HEAD = 128
CONV_CACHE = 8
GROUP = 16
VMEM_LIMIT = 56 * 1024 * 1024

masked_score = -1e30
BF = jnp.bfloat16
F32 = jnp.float32


def mm(a, b):
    return jnp.dot(a, b, preferred_element_type=F32)


def layer_norm(values_in, gain):
    average = jnp.mean(values_in, axis=-1, keepdims=True)
    centered = values_in - average
    spread = jnp.mean(centered * centered, axis=-1, keepdims=True)
    return centered * lax.rsqrt(spread + 1e-05) * gain


def send_slots(new_slot, own_index, peer_count, stream_count):
    target = new_slot // stream_count
    leaving = target != own_index
    index = jnp.arange(stream_count, dtype=jnp.int32)
    earlier = (target[None, :] == target[:, None]) & (index[None, :] < index[:, None])
    position = jnp.sum(earlier.astype(jnp.int32), axis=1)
    bucket = jnp.where(leaving, target * CAP + position, peer_count * CAP)
    return bucket[None, :] == jnp.arange(peer_count * CAP, dtype=jnp.int32)[:, None]


def arrival_slots(old_slot, own_index, slots):
    stream_count = old_slot.shape[0]
    source = old_slot // stream_count
    staying = source == own_index
    earlier = (source[None, :] == source[:, None]) & (old_slot[None, :] < old_slot[:, None])
    position = jnp.sum(earlier.astype(jnp.int32), axis=1)
    arrival = jnp.where(staying, slots, source * CAP + position)
    return arrival, staying


def shift_rows(block, masks):
    for mask, step in zip(masks, (1, 2, 4)):
        block = jnp.where(mask[None], block[step:], block[:-step])
    return block


def project_kernel(x_ref, sw_ref, gain_ref, wq_ref, wk_ref, wv_ref, in_ref, q_ref, k_ref, v_ref):
    x = x_ref[0]
    depth = x.shape[0]
    parts = []
    for g in range(sw_ref.shape[0]):
        part = lax.dot_general(x, sw_ref[g, :depth], (((0,), (0,)), ((), ())), preferred_element_type=F32)
        parts.append(part + sw_ref[g, depth : depth + 1, :].astype(F32))
    inputs = jnp.concatenate(parts, axis=1).astype(BF)
    in_ref[0] = inputs
    normed = layer_norm(inputs.astype(F32), gain_ref[...]).astype(BF)
    q_ref[0] = mm(normed, wq_ref[...]).astype(BF)
    k_ref[0] = mm(normed, wk_ref[...]).astype(BF)
    v_ref[0] = mm(normed, wv_ref[...]).astype(BF)


def project(x, sw, gain, wq, wk, wv):
    frames, depth, streams = x.shape
    width = wq.shape[0]
    local = wq.shape[1]
    whole = lambda shape: pl.BlockSpec(shape, lambda t: (0,) * len(shape))
    row = lambda w: pl.BlockSpec((1, streams, w), lambda t: (t, 0, 0))
    return pl.pallas_call(
        project_kernel,
        grid=(frames,),
        in_specs=[
            pl.BlockSpec((1, depth, streams), lambda t: (t, 0, 0)),
            whole(sw.shape),
            whole(gain.shape),
            whole(wq.shape),
            whole(wk.shape),
            whole(wv.shape),
        ],
        out_specs=[row(width), row(local), row(local), row(local)],
        out_shape=[jax.ShapeDtypeStruct((frames, streams, width), BF)]
        + [jax.ShapeDtypeStruct((frames, streams, local), BF)] * 3,
        compiler_params=pltpu.CompilerParams(vmem_limit_bytes=VMEM_LIMIT),
        name="project",
    )(x, sw, gain, wq, wk, wv)


def attend_kernel(
    has_ref, q_ref, kn_ref, vn_ref, kc_ref, vc_ref, kr_ref, vr_ref, pick_ref, bits_ref, stay_ref,
    colbias_ref, match_ref, ctx_ref, ko_ref, vo_ref, kall, vall,
):
    group = pl.program_id(0)
    local = q_ref.shape[2]
    slots = kr_ref.shape[1]
    span = pick_ref.shape[2] // slots
    kall[0:CACHE] = kc_ref[...]
    vall[0:CACHE] = vc_ref[...]

    @pl.when(has_ref[group] > 0)
    def _():
        stay = (stay_ref[...] > 0.5)[None]
        for first in range(0, CACHE, span):
            count = min(span, CACHE - first)
            pick = pick_ref[0, : count * GROUP, : count * slots]
            for rec, dest in ((kr_ref, kall), (vr_ref, vall)):
                rows = rec[first : first + count].reshape(count * slots, local)
                fetched = mm(pick, rows).astype(BF).reshape(count, GROUP, local)
                dest[first : first + count] = jnp.where(stay, dest[first : first + count], fetched)

    kall[CACHE:TOTAL] = kn_ref[...]
    vall[CACHE:TOTAL] = vn_ref[...]
    bias = match_ref[...] + colbias_ref[0]
    for h in range(local // HEAD):
        lanes = slice(h * HEAD, (h + 1) * HEAD)
        qh = q_ref[:, :, lanes].reshape(FRAMES * GROUP, HEAD)
        kh = kall[:, :, lanes].reshape(TOTAL * GROUP, HEAD)
        vh = vall[:, :, lanes].reshape(TOTAL * GROUP, HEAD)
        scores = lax.dot_general(qh, kh, (((1,), (1,)), ((), ())), preferred_element_type=F32)
        scores = scores * (1.0 / math.sqrt(HEAD)) + bias
        peak = jnp.max(scores, axis=-1, keepdims=True)
        expo = jnp.exp(scores - peak)
        weights = (expo * (1.0 / jnp.sum(expo, axis=-1, keepdims=True))).astype(BF)
        ctx_ref[0, :, lanes] = mm(weights, vh).astype(BF)
    masks = [bits_ref[b] > 0.5 for b in range(3)]
    step = 10
    for src, dst in ((kall, ko_ref), (vall, vo_ref)):
        for first in range(0, CACHE, step):
            dst[first : first + step] = shift_rows(src[first : first + step + FRAMES], masks)


def attend(has, q, kn, vn, kc, vc, kr, vr, pick, bits, stay, colbias, match):
    streams, local = q.shape[1:]
    groups = streams // GROUP
    slots = kr.shape[1]
    block = lambda n: pl.BlockSpec((n, GROUP, local), lambda g, *_: (0, g, 0))
    whole = lambda shape: pl.BlockSpec(shape, lambda g, *_: (0,) * len(shape))
    return pl.pallas_call(
        attend_kernel,
        grid_spec=pltpu.PrefetchScalarGridSpec(
            num_scalar_prefetch=1,
            grid=(groups,),
            in_specs=[
                block(FRAMES), block(FRAMES), block(FRAMES), block(CACHE), block(CACHE),
                whole(kr.shape), whole(vr.shape),
                pl.BlockSpec((1,) + pick.shape[1:], lambda g, *_: (g, 0, 0)),
                block(3),
                pl.BlockSpec((GROUP, local), lambda g, *_: (g, 0)),
                pl.BlockSpec((1, 1, TOTAL * GROUP), lambda g, *_: (g, 0, 0)),
                whole(match.shape),
            ],
            out_specs=[
                pl.BlockSpec((1, FRAMES * GROUP, local), lambda g, *_: (g, 0, 0)), block(CACHE), block(CACHE),
            ],
            scratch_shapes=[pltpu.VMEM((TOTAL, GROUP, local), BF)] * 2,
        ),
        out_shape=[
            jax.ShapeDtypeStruct((groups, FRAMES * GROUP, local), BF),
            jax.ShapeDtypeStruct((CACHE, streams, local), BF),
            jax.ShapeDtypeStruct((CACHE, streams, local), BF),
        ],
        compiler_params=pltpu.CompilerParams(vmem_limit_bytes=VMEM_LIMIT),
        cost_estimate=pl.CostEstimate(flops=1200000000, bytes_accessed=20000000, transcendentals=2500000),
        name="attend",
    )(has, q, kn, vn, kc, vc, kr, vr, pick, bits, stay, colbias, match)


def tail_kernel(
    parts, chunks, ctx_ref, in_ref, wo_ref, gain_ref, wv_ref, wg_ref, conv_ref, bits_ref, dk_ref, scale_ref,
    bias_ref, wc_ref, valid_ref, enc_ref, co_ref, ctx_all, act_all, middle_own, middle_now, conv_all,
    ctx_send, ctx_recv, act_send, act_recv,
):
    me = lax.axis_index("enc")
    local = ctx_ref.shape[2]
    width = in_ref.shape[2]
    rows = FRAMES * GROUP
    last = parts - 1
    right = lax.rem(me + 1, parts)
    left = lax.rem(me + parts - 1, parts)
    mesh_ids = pl.DeviceIdType.MESH

    barrier = pltpu.get_barrier_semaphore()

    @pl.when(me > 0)
    def _():
        pl.semaphore_signal(barrier, inc=1, device_id={"enc": left}, device_id_type=mesh_ids)

    @pl.when(me < last)
    def _():
        pl.semaphore_signal(barrier, inc=1, device_id={"enc": right}, device_id_type=mesh_ids)

    inner = (me > 0) & (me < last)

    @pl.when(inner)
    def _():
        pl.semaphore_wait(barrier, 2)

    @pl.when(jnp.logical_not(inner))
    def _():
        pl.semaphore_wait(barrier, 1)

    def hop(line, source, chunk, way):
        buffer, send, recv = line
        return pltpu.make_async_remote_copy(
            src_ref=buffer.at[source, chunk],
            dst_ref=buffer.at[source, chunk],
            send_sem=send.at[way, source, chunk],
            recv_sem=recv.at[source, chunk],
            device_id={"enc": (right, left)[way]},
            device_id_type=mesh_ids,
        )

    def send_own(line, chunk):
        @pl.when(me < last)
        def _():
            hop(line, me, chunk, 0).start()

        @pl.when(me > 0)
        def _():
            hop(line, me, chunk, 1).start()

    def pass_on(line, chunk, distance):
        @pl.when(me >= distance)
        def _():
            copy = hop(line, me - distance, chunk, 0)
            copy.wait_recv()

            @pl.when(me < last)
            def _():
                copy.start()

        @pl.when(me + distance <= last)
        def _():
            copy = hop(line, me + distance, chunk, 1)
            copy.wait_recv()

            @pl.when(me > 0)
            def _():
                copy.start()

    def sent(line, chunk):
        for source in range(parts):
            @pl.when((me >= source) & (me < last))
            def _():
                hop(line, source, chunk, 0).wait_send()

            @pl.when((me <= source) & (me > 0))
            def _():
                hop(line, source, chunk, 1).wait_send()

    def convolve(chunk):
        here = pl.ds(pl.multiple_of(chunk * GROUP, GROUP), GROUP)
        attended = jnp.zeros((rows, width), F32)
        for g in range(parts):
            share = mm(ctx_all[g, chunk], wo_ref[g * local : (g + 1) * local])
            attended = attended + share.astype(BF).astype(F32)
        middle = (in_ref[:, here, :].reshape(rows, width).astype(F32) + attended).astype(BF)
        middle_now[...] = middle
        middle_own[chunk] = middle_now[:, pl.ds(pl.multiple_of(me * local, local), local)]
        normed = layer_norm(middle.astype(F32), gain_ref[...]).astype(BF)
        gated = (mm(normed, wv_ref[...]) * jax.nn.sigmoid(mm(normed, wg_ref[...]))).astype(BF)
        conv_all[0:CONV_CACHE] = conv_ref[:, here, :]
        conv_all[CONV_CACHE:] = gated.reshape(FRAMES, GROUP, local)
        for t in range(FRAMES):
            total = jnp.zeros((GROUP, local), F32)
            for k in range(KERNEL):
                total = total + dk_ref[k : k + 1, :] * conv_all[t + k].astype(F32)
            shaped = total * scale_ref[...] + bias_ref[...]
            active = (shaped * jax.nn.sigmoid(shaped)).astype(BF)
            act_all[me, chunk, t * GROUP : (t + 1) * GROUP] = active
        masks = [bits_ref[b, here, :] > 0.5 for b in range(3)]
        co_ref[:, here, :] = shift_rows(conv_all[...], masks)

    def finish(chunk):
        here = pl.ds(pl.multiple_of(chunk * GROUP, GROUP), GROUP)
        total = jnp.zeros((rows, local), F32)
        for g in range(parts):
            share = mm(act_all[g, chunk], wc_ref[g * local : (g + 1) * local])
            total = total + share.astype(BF).astype(F32)
        total = (total + middle_own[chunk].astype(F32)).reshape(FRAMES, GROUP, local)
        valid = valid_ref[here, :]
        for t in range(FRAMES):
            enc_ref[t, here, :] = jnp.where(valid > t + 0.5, total[t], 0.0).astype(BF)

    ctx_all[me] = ctx_ref[...]
    ctx_line = (ctx_all, ctx_send, ctx_recv)
    act_line = (act_all, act_send, act_recv)

    def turn(step, carry):
        def at(lag, action):
            chunk = step - lag

            @pl.when((chunk >= 0) & (chunk < chunks))
            def _():
                action(chunk)

        def middle_part(chunk):
            pass_on(ctx_line, chunk, last)
            convolve(chunk)
            send_own(act_line, chunk)

        def end_part(chunk):
            pass_on(act_line, chunk, last)
            finish(chunk)

        at(0, lambda c: send_own(ctx_line, c))
        for d in range(1, last):
            at(d, lambda c, d=d: pass_on(ctx_line, c, d))
        at(last, middle_part)
        for d in range(1, last):
            at(last + d, lambda c, d=d: pass_on(act_line, c, d))
        at(2 * last, end_part)
        return carry

    lax.fori_loop(0, chunks + 2 * last, turn, 0)

    def drain(chunk, carry):
        sent(ctx_line, chunk)
        sent(act_line, chunk)
        return carry

    lax.fori_loop(0, chunks, drain, 0)


def tail(parts, ctx, inputs, wo, gain, wv, wg, conv, bits, dk, scale, bias, wc, valid_wide):
    chunks, rows, local = ctx.shape
    frames, streams, width = inputs.shape
    vmem = pl.BlockSpec(memory_space=pltpu.VMEM)
    return pl.pallas_call(
        functools.partial(tail_kernel, parts, chunks),
        in_specs=[vmem] * 13,
        out_specs=[vmem] * 2,
        out_shape=[
            jax.ShapeDtypeStruct((frames, streams, local), BF),
            jax.ShapeDtypeStruct((CONV_CACHE, streams, local), BF),
        ],
        scratch_shapes=[
            pltpu.VMEM((parts, chunks, rows, local), BF),
            pltpu.VMEM((parts, chunks, rows, local), BF),
            pltpu.VMEM((chunks, rows, local), BF),
            pltpu.VMEM((rows, width), BF),
            pltpu.VMEM((CONV_CACHE + frames, GROUP, local), BF),
            pltpu.SemaphoreType.DMA((2, parts, chunks)),
            pltpu.SemaphoreType.DMA((parts, chunks)),
            pltpu.SemaphoreType.DMA((2, parts, chunks)),
            pltpu.SemaphoreType.DMA((parts, chunks)),
        ],
        compiler_params=pltpu.CompilerParams(
            vmem_limit_bytes=VMEM_LIMIT, collective_id=0, has_side_effects=True
        ),
        cost_estimate=pl.CostEstimate(flops=4000000000, bytes_accessed=10000000, transcendentals=1000000),
        name="tail",
    )(ctx, inputs, wo, gain, wv, wg, conv, bits, dk, scale, bias, wc, valid_wide)


def on_device(
    spectra,
    sub_weight,
    sub_bias,
    key_cache,
    value_cache,
    conv_cache,
    new_slot,
    old_slot,
    valid_new,
    cache_fill,
    ln1_gain,
    w_query,
    w_key,
    w_value,
    w_attn_out,
    ln2_gain,
    w_glu_value,
    w_glu_gate,
    depth_kernel,
    norm_scale,
    norm_shift,
    w_conv_out,
):
    peer_count = lax.axis_size("front")
    own_index = lax.axis_index("front")
    streams = spectra.shape[0]
    local = w_query.shape[1]
    slots = peer_count * CAP
    mels = spectra.shape[2]

    bias_rows = jnp.broadcast_to(sub_bias[None], (16, local))
    sub_full = lax.all_gather(jnp.concatenate([sub_weight, bias_rows], axis=0), "enc")
    attn_full = lax.all_gather(w_attn_out, "enc", tiled=True)
    conv_cols = lax.all_to_all(w_conv_out, "enc", split_axis=1, concat_axis=0, tiled=True)

    leaving = send_slots(new_slot, own_index, peer_count, streams).astype(BF)
    arrival, staying = arrival_slots(old_slot, own_index, slots)
    arriving = (arrival[:, None] == jnp.arange(slots, dtype=jnp.int32)[None, :]).astype(BF)

    x = spectra.transpose(1, 2, 0).reshape(FRAMES * SUB * mels, streams)
    x_send = lax.dot_general(leaving, x, (((1,), (1,)), ((), ())), preferred_element_type=F32).astype(BF)
    x_recv = lax.all_to_all(x_send, "front", split_axis=0, concat_axis=0, tiled=True)
    x_moved = lax.dot_general(x_recv, arriving, (((0,), (1,)), ((), ())), preferred_element_type=F32).astype(BF)
    x_new = jnp.where(staying[None, :], x, x_moved).reshape(FRAMES, SUB * mels, streams)

    keys = key_cache.transpose(1, 0, 2)
    values = value_cache.transpose(1, 0, 2)
    conv = conv_cache.transpose(1, 0, 2)
    choose = lambda a: jnp.einsum("rs,jsc->rjc", leaving, a, preferred_element_type=F32).astype(BF)
    bundle = jnp.concatenate([choose(keys), choose(values), choose(conv)], axis=1)
    bundle, conv_cols = lax.optimization_barrier((bundle, conv_cols))
    recv = lax.all_to_all(bundle, "front", split_axis=0, concat_axis=0, tiled=True).transpose(1, 0, 2)
    keys_recv, values_recv = recv[:CACHE], recv[CACHE : 2 * CACHE]
    conv_moved = jnp.einsum(
        "sr,jrc->jsc", arriving, recv[2 * CACHE :], preferred_element_type=F32
    ).astype(BF)
    conv_old = jnp.where(staying[None, :, None], conv, conv_moved)

    groups = streams // GROUP
    span = max(1, 256 // slots)
    wanted = jnp.tile(arrival.reshape(groups, GROUP), (1, span))
    spot = jnp.arange(span * slots, dtype=jnp.int32)
    block_of = jnp.arange(span * GROUP, dtype=jnp.int32) // GROUP
    pick = (
        (wanted[:, :, None] == (spot % slots)[None, None, :])
        & (block_of[:, None] == (spot // slots)[None, :])[None]
    ).astype(BF)
    has = jnp.sum((~staying).astype(jnp.int32).reshape(groups, GROUP), axis=1)
    valid_wide = jnp.broadcast_to(valid_new.astype(F32)[:, None], (streams, local))
    bits = jnp.stack([(valid_new >> b) & 1 for b in range(3)]).astype(BF)
    bits = jnp.broadcast_to(bits[:, :, None], (3, streams, local))
    stay_wide = jnp.broadcast_to(staying.astype(BF)[:, None], (streams, local))
    position = jnp.arange(TOTAL, dtype=jnp.int32)[:, None]
    cache_ok = (position < CACHE) & (position >= CACHE - cache_fill[None, :])
    new_ok = (position >= CACHE) & (position - CACHE < valid_new[None, :])
    colbias = jnp.where(cache_ok | new_ok, 0.0, masked_score).astype(F32)
    colbias = colbias.reshape(TOTAL, groups, GROUP).transpose(1, 0, 2).reshape(groups, 1, TOTAL * GROUP)
    row_of = jnp.arange(FRAMES * GROUP, dtype=jnp.int32) % GROUP
    col_of = jnp.arange(TOTAL * GROUP, dtype=jnp.int32) % GROUP
    match = jnp.where(row_of[:, None] == col_of[None, :], 0.0, masked_score).astype(F32)

    inputs, queries, key_new, value_new = project(
        x_new, sub_full, ln1_gain[None], w_query, w_key, w_value
    )
    context, key_out, value_out = attend(
        has, queries, key_new, value_new, keys, values, keys_recv, values_recv, pick, bits, stay_wide,
        colbias, match,
    )
    encoded, conv_out = tail(
        lax.axis_size("enc"), context, inputs, attn_full, ln2_gain[None], w_glu_value, w_glu_gate, conv_old,
        bits, depth_kernel, norm_scale[None], norm_shift[None], conv_cols, valid_wide,
    )
    back = lambda a: a.transpose(1, 0, 2)
    return back(encoded), back(key_out), back(value_out), back(conv_out)


def solution(mesh):
    in_specs = (
        P("front", None, None),
        P(None, "enc"),
        P("enc"),
        P("front", None, "enc"),
        P("front", None, "enc"),
        P("front", None, "enc"),
        P("front"),
        P("front"),
        P("front"),
        P("front"),
        P(),
        P(None, "enc"),
        P(None, "enc"),
        P(None, "enc"),
        P("enc", None),
        P(),
        P(None, "enc"),
        P(None, "enc"),
        P(None, "enc"),
        P("enc"),
        P("enc"),
        P("enc", None),
    )
    out_specs = (P("front", None, "enc"),) * 4
    return jax.shard_map(
        on_device, mesh=mesh, in_specs=in_specs, out_specs=out_specs, check_vma=False
    )
```

```python
import functools
import math

import jax
import jax.numpy as jnp
from jax import lax
from jax.experimental import pallas as pl
from jax.experimental.pallas import tpu as pltpu
import numpy as np
from jax.sharding import PartitionSpec as P

KERNEL = 9
SUB = 8
FRAMES = 7
CACHE = 70
TOTAL = CACHE + FRAMES
CAP = 2
HEAD = 128
CONV_CACHE = 8
GROUP = 16
VMEM_LIMIT = 56 * 1024 * 1024

masked_score = -1e30
BF = jnp.bfloat16
F32 = jnp.float32


def mm(a, b):
    return jnp.dot(a, b, preferred_element_type=F32)


def layer_norm(values_in, gain):
    average = jnp.mean(values_in, axis=-1, keepdims=True)
    centered = values_in - average
    spread = jnp.mean(centered * centered, axis=-1, keepdims=True)
    return centered * lax.rsqrt(spread + 1e-05) * gain


def send_slots(new_slot, own_index, peer_count, stream_count):
    target = lax.div(new_slot, stream_count)
    leaving = target != own_index
    index = jnp.arange(stream_count, dtype=jnp.int32)
    earlier = (target[None, :] == target[:, None]) & (index[None, :] < index[:, None])
    position = jnp.sum(earlier.astype(jnp.int32), axis=1)
    bucket = jnp.where(leaving, target * CAP + position, peer_count * CAP)
    return bucket[None, :] == jnp.arange(peer_count * CAP, dtype=jnp.int32)[:, None]


def arrival_slots(old_slot, own_index, slots):
    stream_count = old_slot.shape[0]
    source = lax.div(old_slot, stream_count)
    staying = source == own_index
    earlier = (source[None, :] == source[:, None]) & (old_slot[None, :] < old_slot[:, None])
    position = jnp.sum(earlier.astype(jnp.int32), axis=1)
    arrival = jnp.where(staying, slots, source * CAP + position)
    return arrival, staying


def shift_rows(block, masks):
    for mask, step in zip(masks, (1, 2, 4)):
        block = jnp.where(mask[None], block[step:], block[:-step])
    return block


def project_kernel(x_ref, sw_ref, gain_ref, wq_ref, wk_ref, wv_ref, in_ref, q_ref, k_ref, v_ref):
    x = x_ref[0]
    depth = x.shape[0]
    parts = []
    for g in range(sw_ref.shape[0]):
        part = lax.dot_general(x, sw_ref[g, :depth], (((0,), (0,)), ((), ())), preferred_element_type=F32)
        parts.append(part + sw_ref[g, depth : depth + 1, :].astype(F32))
    inputs = jnp.concatenate(parts, axis=1).astype(BF)
    in_ref[0] = inputs
    normed = layer_norm(inputs.astype(F32), gain_ref[...]).astype(BF)
    q_ref[0] = mm(normed, wq_ref[...]).astype(BF)
    k_ref[0] = mm(normed, wk_ref[...]).astype(BF)
    v_ref[0] = mm(normed, wv_ref[...]).astype(BF)


def project(x, sw, gain, wq, wk, wv):
    frames, depth, streams = x.shape
    width = wq.shape[0]
    local = wq.shape[1]
    whole = lambda shape: pl.BlockSpec(shape, lambda t: (0,) * len(shape))
    row = lambda w: pl.BlockSpec((1, streams, w), lambda t: (t, 0, 0))
    return pl.pallas_call(
        project_kernel,
        grid=(frames,),
        in_specs=[
            pl.BlockSpec((1, depth, streams), lambda t: (t, 0, 0)),
            whole(sw.shape),
            whole(gain.shape),
            whole(wq.shape),
            whole(wk.shape),
            whole(wv.shape),
        ],
        out_specs=[row(width), row(local), row(local), row(local)],
        out_shape=[jax.ShapeDtypeStruct((frames, streams, width), BF)]
        + [jax.ShapeDtypeStruct((frames, streams, local), BF)] * 3,
        compiler_params=pltpu.CompilerParams(vmem_limit_bytes=VMEM_LIMIT),
        cost_estimate=pl.CostEstimate(flops=2600000000, bytes_accessed=25000000, transcendentals=1000),
        name="project",
    )(x, sw, gain, wq, wk, wv)


def attend_kernel(
    has_ref, q_ref, kn_ref, vn_ref, kc_ref, vc_ref, kr_ref, vr_ref, pick_ref, bits_ref, stay_ref,
    colbias_ref, match_ref, ctx_ref, ko_ref, vo_ref, kall, vall,
):
    group = pl.program_id(0)
    local = q_ref.shape[2]
    slots = kr_ref.shape[1]
    span = pick_ref.shape[2] // slots
    kall[0:CACHE] = kc_ref[...]
    vall[0:CACHE] = vc_ref[...]

    @pl.when(has_ref[group] > 0)
    def _():
        stay = (stay_ref[...] > 0.5)[None]
        for first in range(0, CACHE, span):
            count = min(span, CACHE - first)
            pick = pick_ref[0, : count * GROUP, : count * slots]
            for rec, dest in ((kr_ref, kall), (vr_ref, vall)):
                rows = rec[first : first + count].reshape(count * slots, local)
                fetched = mm(pick, rows).astype(BF).reshape(count, GROUP, local)
                dest[first : first + count] = jnp.where(stay, dest[first : first + count], fetched)

    kall[CACHE:TOTAL] = kn_ref[...]
    vall[CACHE:TOTAL] = vn_ref[...]
    bias = match_ref[...] + colbias_ref[0]
    for h in range(local // HEAD):
        lanes = slice(h * HEAD, (h + 1) * HEAD)
        qh = q_ref[:, :, lanes].reshape(FRAMES * GROUP, HEAD)
        kh = kall[:, :, lanes].reshape(TOTAL * GROUP, HEAD)
        vh = vall[:, :, lanes].reshape(TOTAL * GROUP, HEAD)
        scores = lax.dot_general(qh, kh, (((1,), (1,)), ((), ())), preferred_element_type=F32)
        scores = scores * (1.0 / math.sqrt(HEAD)) + bias
        peak = jnp.max(scores, axis=-1, keepdims=True)
        expo = jnp.exp(scores - peak)
        weights = (expo * (1.0 / jnp.sum(expo, axis=-1, keepdims=True))).astype(BF)
        ctx_ref[0, :, lanes] = mm(weights, vh).astype(BF)
    masks = [bits_ref[b] > 0.5 for b in range(3)]
    step = 10
    for src, dst in ((kall, ko_ref), (vall, vo_ref)):
        for first in range(0, CACHE, step):
            dst[first : first + step] = shift_rows(src[first : first + step + FRAMES], masks)


def attend(has, q, kn, vn, kc, vc, kr, vr, pick, bits, stay, colbias, match):
    streams, local = q.shape[1:]
    groups = streams // GROUP
    slots = kr.shape[1]
    block = lambda n: pl.BlockSpec((n, GROUP, local), lambda g, *_: (0, g, 0))
    whole = lambda shape: pl.BlockSpec(shape, lambda g, *_: (0,) * len(shape))
    return pl.pallas_call(
        attend_kernel,
        grid_spec=pltpu.PrefetchScalarGridSpec(
            num_scalar_prefetch=1,
            grid=(groups,),
            in_specs=[
                block(FRAMES), block(FRAMES), block(FRAMES), block(CACHE), block(CACHE),
                whole(kr.shape), whole(vr.shape),
                pl.BlockSpec((1,) + pick.shape[1:], lambda g, *_: (g, 0, 0)),
                block(3),
                pl.BlockSpec((GROUP, local), lambda g, *_: (g, 0)),
                pl.BlockSpec((1, 1, TOTAL * GROUP), lambda g, *_: (g, 0, 0)),
                whole(match.shape),
            ],
            out_specs=[
                pl.BlockSpec((1, FRAMES * GROUP, local), lambda g, *_: (g, 0, 0)), block(CACHE), block(CACHE),
            ],
            scratch_shapes=[pltpu.VMEM((TOTAL, GROUP, local), BF)] * 2,
        ),
        out_shape=[
            jax.ShapeDtypeStruct((groups, FRAMES * GROUP, local), BF),
            jax.ShapeDtypeStruct((CACHE, streams, local), BF),
            jax.ShapeDtypeStruct((CACHE, streams, local), BF),
        ],
        compiler_params=pltpu.CompilerParams(vmem_limit_bytes=VMEM_LIMIT),
        cost_estimate=pl.CostEstimate(flops=1200000000, bytes_accessed=20000000, transcendentals=2500000),
        name="attend",
    )(has, q, kn, vn, kc, vc, kr, vr, pick, bits, stay, colbias, match)


def tail_kernel(
    parts, chunks, ctx_ref, in_ref, wo_ref, gain_ref, wv_ref, wg_ref, conv_ref, bits_ref, dk_ref, scale_ref,
    bias_ref, wc_ref, valid_ref, enc_ref, co_ref, ctx_all, act_all, middle_own, middle_now, conv_all,
    ctx_send, ctx_recv, act_send, act_recv,
):
    me = lax.axis_index("enc")
    local = ctx_ref.shape[2]
    width = in_ref.shape[2]
    rows = FRAMES * GROUP
    last = parts - 1
    right = lax.rem(me + 1, parts)
    left = lax.rem(me + parts - 1, parts)
    mesh_ids = pl.DeviceIdType.MESH

    barrier = pltpu.get_barrier_semaphore()

    @pl.when(me > 0)
    def _():
        pl.semaphore_signal(barrier, inc=1, device_id={"enc": left}, device_id_type=mesh_ids)

    @pl.when(me < last)
    def _():
        pl.semaphore_signal(barrier, inc=1, device_id={"enc": right}, device_id_type=mesh_ids)

    inner = (me > 0) & (me < last)

    @pl.when(inner)
    def _():
        pl.semaphore_wait(barrier, 2)

    @pl.when(jnp.logical_not(inner))
    def _():
        pl.semaphore_wait(barrier, 1)

    def hop(line, source, chunk, way):
        buffer, send, recv = line
        return pltpu.make_async_remote_copy(
            src_ref=buffer.at[source, chunk],
            dst_ref=buffer.at[source, chunk],
            send_sem=send.at[way, source, chunk],
            recv_sem=recv.at[source, chunk],
            device_id={"enc": (right, left)[way]},
            device_id_type=mesh_ids,
        )

    def send_own(line, chunk):
        @pl.when(me < last)
        def _():
            hop(line, me, chunk, 0).start()

        @pl.when(me > 0)
        def _():
            hop(line, me, chunk, 1).start()

    def pass_on(line, chunk, distance):
        @pl.when(me >= distance)
        def _():
            copy = hop(line, me - distance, chunk, 0)
            copy.wait_recv()

            @pl.when(me < last)
            def _():
                copy.start()

        @pl.when(me + distance <= last)
        def _():
            copy = hop(line, me + distance, chunk, 1)
            copy.wait_recv()

            @pl.when(me > 0)
            def _():
                copy.start()

    def sent(line, chunk):
        for source in range(parts):
            @pl.when((me >= source) & (me < last))
            def _():
                hop(line, source, chunk, 0).wait_send()

            @pl.when((me <= source) & (me > 0))
            def _():
                hop(line, source, chunk, 1).wait_send()

    def convolve(chunk):
        here = pl.ds(pl.multiple_of(chunk * GROUP, GROUP), GROUP)
        attended = jnp.zeros((rows, width), F32)
        for g in range(parts):
            share = mm(ctx_all[g, chunk], wo_ref[g * local : (g + 1) * local])
            attended = attended + share.astype(BF).astype(F32)
        middle = (in_ref[:, here, :].reshape(rows, width).astype(F32) + attended).astype(BF)
        middle_now[...] = middle
        middle_own[chunk] = middle_now[:, pl.ds(pl.multiple_of(me * local, local), local)]
        normed = layer_norm(middle.astype(F32), gain_ref[...]).astype(BF)
        gated = (mm(normed, wv_ref[...]) * jax.nn.sigmoid(mm(normed, wg_ref[...]))).astype(BF)
        conv_all[0:CONV_CACHE] = conv_ref[:, here, :]
        conv_all[CONV_CACHE:] = gated.reshape(FRAMES, GROUP, local)
        for t in range(FRAMES):
            total = jnp.zeros((GROUP, local), F32)
            for k in range(KERNEL):
                total = total + dk_ref[k : k + 1, :] * conv_all[t + k].astype(F32)
            shaped = total * scale_ref[...] + bias_ref[...]
            active = (shaped * jax.nn.sigmoid(shaped)).astype(BF)
            act_all[me, chunk, t * GROUP : (t + 1) * GROUP] = active
        masks = [bits_ref[b, here, :] > 0.5 for b in range(3)]
        co_ref[:, here, :] = shift_rows(conv_all[...], masks)

    def finish(chunk):
        here = pl.ds(pl.multiple_of(chunk * GROUP, GROUP), GROUP)
        total = jnp.zeros((rows, local), F32)
        for g in range(parts):
            share = mm(act_all[g, chunk], wc_ref[lax.rem(me + parts - g, parts)])
            total = total + share.astype(BF).astype(F32)
        total = (total + middle_own[chunk].astype(F32)).reshape(FRAMES, GROUP, local)
        valid = valid_ref[here, :]
        for t in range(FRAMES):
            enc_ref[t, here, :] = jnp.where(valid > t + 0.5, total[t], 0.0).astype(BF)

    ctx_all[me] = ctx_ref[...]
    ctx_line = (ctx_all, ctx_send, ctx_recv)
    act_line = (act_all, act_send, act_recv)

    def turn(step, carry):
        def at(lag, action):
            chunk = step - lag

            @pl.when((chunk >= 0) & (chunk < chunks))
            def _():
                action(chunk)

        def middle_part(chunk):
            pass_on(ctx_line, chunk, last)
            convolve(chunk)
            send_own(act_line, chunk)

        def end_part(chunk):
            pass_on(act_line, chunk, last)
            finish(chunk)

        at(0, lambda c: send_own(ctx_line, c))
        for d in range(1, last):
            at(d, lambda c, d=d: pass_on(ctx_line, c, d))
        at(last, middle_part)
        for d in range(1, last):
            at(last + d, lambda c, d=d: pass_on(act_line, c, d))
        at(2 * last, end_part)
        return carry

    lax.fori_loop(0, chunks + 2 * last, turn, 0)

    def drain(chunk, carry):
        sent(ctx_line, chunk)
        sent(act_line, chunk)
        return carry

    lax.fori_loop(0, chunks, drain, 0)


def tail(parts, ctx, inputs, wo, gain, wv, wg, conv, bits, dk, scale, bias, wc, valid_wide):
    chunks, rows, local = ctx.shape
    frames, streams, width = inputs.shape
    vmem = pl.BlockSpec(memory_space=pltpu.VMEM)
    return pl.pallas_call(
        functools.partial(tail_kernel, parts, chunks),
        in_specs=[vmem] * 13,
        out_specs=[vmem] * 2,
        out_shape=[
            jax.ShapeDtypeStruct((frames, streams, local), BF),
            jax.ShapeDtypeStruct((CONV_CACHE, streams, local), BF),
        ],
        scratch_shapes=[
            pltpu.VMEM((parts, chunks, rows, local), BF),
            pltpu.VMEM((parts, chunks, rows, local), BF),
            pltpu.VMEM((chunks, rows, local), BF),
            pltpu.VMEM((rows, width), BF),
            pltpu.VMEM((CONV_CACHE + frames, GROUP, local), BF),
            pltpu.SemaphoreType.DMA((2, parts, chunks)),
            pltpu.SemaphoreType.DMA((parts, chunks)),
            pltpu.SemaphoreType.DMA((2, parts, chunks)),
            pltpu.SemaphoreType.DMA((parts, chunks)),
        ],
        compiler_params=pltpu.CompilerParams(
            vmem_limit_bytes=VMEM_LIMIT, collective_id=0, has_side_effects=True
        ),
        cost_estimate=pl.CostEstimate(flops=4000000000, bytes_accessed=10000000, transcendentals=1000000),
        name="tail",
    )(ctx, inputs, wo, gain, wv, wg, conv, bits, dk, scale, bias, wc, valid_wide)


def on_device(
    spectra,
    sub_weight,
    sub_bias,
    key_cache,
    value_cache,
    conv_cache,
    new_slot,
    old_slot,
    valid_new,
    cache_fill,
    ln1_gain,
    w_query,
    w_key,
    w_value,
    w_attn_out,
    ln2_gain,
    w_glu_value,
    w_glu_gate,
    depth_kernel,
    norm_scale,
    norm_shift,
    w_conv_out,
):
    peer_count = lax.axis_size("front")
    own_index = lax.axis_index("front")
    streams = spectra.shape[0]
    local = w_query.shape[1]
    slots = peer_count * CAP
    mels = spectra.shape[2]

    bias_rows = jnp.broadcast_to(sub_bias[None], (16, local))
    sub_full = lax.all_gather(jnp.concatenate([sub_weight, bias_rows], axis=0), "enc")
    attn_full = lax.all_gather(w_attn_out, "enc", tiled=True)
    parts = lax.axis_size("enc")
    member = lax.axis_index("enc")
    conv_cols = []
    for shift in range(parts):
        piece = lax.dynamic_slice_in_dim(w_conv_out, lax.rem(member + shift, parts) * local, local, 1)
        if shift:
            piece = lax.ppermute(piece, "enc", [(m, (m + shift) % parts) for m in range(parts)])
        conv_cols.append(piece)
    conv_cols = jnp.stack(conv_cols)

    leaving = send_slots(new_slot, own_index, peer_count, streams).astype(BF)
    arrival, staying = arrival_slots(old_slot, own_index, slots)
    arriving = (arrival[:, None] == jnp.arange(slots, dtype=jnp.int32)[None, :]).astype(BF)

    x = spectra.transpose(1, 2, 0).reshape(FRAMES * SUB * mels, streams)
    x_send = lax.dot_general(leaving, x, (((1,), (1,)), ((), ())), preferred_element_type=F32).astype(BF)
    x_recv = lax.all_to_all(x_send, "front", split_axis=0, concat_axis=0, tiled=True)
    x_moved = lax.dot_general(x_recv, arriving, (((0,), (1,)), ((), ())), preferred_element_type=F32).astype(BF)
    x_new = jnp.where(staying[None, :], x, x_moved).reshape(FRAMES, SUB * mels, streams)

    keys = key_cache.transpose(1, 0, 2)
    values = value_cache.transpose(1, 0, 2)
    conv = conv_cache.transpose(1, 0, 2)
    choose = lambda a: jnp.einsum("rs,jsc->rjc", leaving, a, preferred_element_type=F32).astype(BF)
    bundle = jnp.concatenate([choose(keys), choose(values), choose(conv)], axis=1)
    recv = lax.all_to_all(bundle, "front", split_axis=0, concat_axis=0, tiled=True)
    inputs, queries, key_new, value_new = project(
        x_new, sub_full, ln1_gain[None], w_query, w_key, w_value
    )
    recv, queries = lax.optimization_barrier((recv, queries))
    recv = recv.transpose(1, 0, 2)
    keys_recv, values_recv = recv[:CACHE], recv[CACHE : 2 * CACHE]
    conv_moved = jnp.einsum(
        "sr,jrc->jsc", arriving, recv[2 * CACHE :], preferred_element_type=F32
    ).astype(BF)
    conv_old = jnp.where(staying[None, :, None], conv, conv_moved)

    groups = streams // GROUP
    span = max(1, 256 // slots)
    wanted = jnp.tile(arrival.reshape(groups, GROUP), (1, span))
    spot = np.arange(span * slots, dtype=np.int32)
    block_of = np.arange(span * GROUP, dtype=np.int32) // GROUP
    slot_in = np.where(block_of[:, None] == (spot // slots)[None, :], (spot % slots)[None, :], -1)
    pick = (wanted[:, :, None] == slot_in.astype(np.int32)[None]).astype(BF)
    has = jnp.sum((~staying).astype(jnp.int32).reshape(groups, GROUP), axis=1)
    valid_wide = jnp.broadcast_to(valid_new.astype(F32)[:, None], (streams, local))
    bits = jnp.stack([(valid_new >> b) & 1 for b in range(3)]).astype(BF)
    bits = jnp.broadcast_to(bits[:, :, None], (3, streams, local))
    stay_wide = jnp.broadcast_to(staying.astype(BF)[:, None], (streams, local))
    col = np.arange(TOTAL * GROUP, dtype=np.int32)
    row = np.arange(FRAMES * GROUP, dtype=np.int32)
    least = jnp.tile((CACHE - cache_fill).reshape(groups, GROUP), (1, TOTAL))
    most = jnp.tile((CACHE + valid_new).reshape(groups, GROUP), (1, TOTAL))
    spread_col = (col // GROUP)[None, :]
    colbias = jnp.where((spread_col >= least) & (spread_col < most), 0.0, masked_score)
    colbias = colbias.astype(F32)[:, None, :]
    match = jnp.asarray(
        np.where((row % GROUP)[:, None] == (col % GROUP)[None, :], 0.0, masked_score).astype(np.float32)
    )

    context, key_out, value_out = attend(
        has, queries, key_new, value_new, keys, values, keys_recv, values_recv, pick, bits, stay_wide,
        colbias, match,
    )
    encoded, conv_out = tail(
        parts, context, inputs, attn_full, ln2_gain[None], w_glu_value, w_glu_gate, conv_old,
        bits, depth_kernel, norm_scale[None], norm_shift[None], conv_cols, valid_wide,
    )
    back = lambda a: a.transpose(1, 0, 2)
    return back(encoded), back(key_out), back(value_out), back(conv_out)


def solution(mesh):
    in_specs = (
        P("front", None, None),
        P(None, "enc"),
        P("enc"),
        P("front", None, "enc"),
        P("front", None, "enc"),
        P("front", None, "enc"),
        P("front"),
        P("front"),
        P("front"),
        P("front"),
        P(),
        P(None, "enc"),
        P(None, "enc"),
        P(None, "enc"),
        P("enc", None),
        P(),
        P(None, "enc"),
        P(None, "enc"),
        P(None, "enc"),
        P("enc"),
        P("enc"),
        P("enc", None),
    )
    out_specs = (P("front", None, "enc"),) * 4
    return jax.shard_map(
        on_device, mesh=mesh, in_specs=in_specs, out_specs=out_specs, check_vma=False
    )
```

```python
import functools
import math

import jax
import jax.numpy as jnp
from jax import lax
from jax.experimental import pallas as pl
from jax.experimental.pallas import tpu as pltpu
import numpy as np
from jax.sharding import PartitionSpec as P

KERNEL = 9
SUB = 8
FRAMES = 7
CACHE = 70
TOTAL = CACHE + FRAMES
CAP = 2
HEAD = 128
CONV_CACHE = 8
GROUP = 16
VMEM_LIMIT = 56 * 1024 * 1024

masked_score = -1e30
BF = jnp.bfloat16
F32 = jnp.float32


def mm(a, b):
    return jnp.dot(a, b, preferred_element_type=F32)


def layer_norm(values_in, gain):
    average = jnp.mean(values_in, axis=-1, keepdims=True)
    centered = values_in - average
    spread = jnp.mean(centered * centered, axis=-1, keepdims=True)
    return centered * lax.rsqrt(spread + 1e-05) * gain


def send_slots(new_slot, own_index, peer_count, stream_count):
    target = lax.div(new_slot, stream_count)
    leaving = target != own_index
    index = jnp.arange(stream_count, dtype=jnp.int32)
    earlier = (target[None, :] == target[:, None]) & (index[None, :] < index[:, None])
    position = jnp.sum(earlier.astype(jnp.int32), axis=1)
    bucket = jnp.where(leaving, target * CAP + position, peer_count * CAP)
    return bucket[None, :] == jnp.arange(peer_count * CAP, dtype=jnp.int32)[:, None]


def arrival_slots(old_slot, own_index, slots):
    stream_count = old_slot.shape[0]
    source = lax.div(old_slot, stream_count)
    staying = source == own_index
    earlier = (source[None, :] == source[:, None]) & (old_slot[None, :] < old_slot[:, None])
    position = jnp.sum(earlier.astype(jnp.int32), axis=1)
    arrival = jnp.where(staying, slots, source * CAP + position)
    return arrival, staying


def shift_rows(block, masks):
    for mask, step in zip(masks, (1, 2, 4)):
        block = jnp.where(mask[None], block[step:], block[:-step])
    return block


def project_kernel(x_ref, sw_ref, gain_ref, wq_ref, wk_ref, wv_ref, in_ref, q_ref, k_ref, v_ref):
    x = x_ref[0]
    depth = x.shape[0]
    parts = []
    for g in range(sw_ref.shape[0]):
        part = lax.dot_general(x, sw_ref[g, :depth], (((0,), (0,)), ((), ())), preferred_element_type=F32)
        parts.append(part + sw_ref[g, depth : depth + 1, :].astype(F32))
    inputs = jnp.concatenate(parts, axis=1).astype(BF)
    in_ref[0] = inputs
    normed = layer_norm(inputs.astype(F32), gain_ref[...]).astype(BF)
    q_ref[0] = mm(normed, wq_ref[...]).astype(BF)
    k_ref[0] = mm(normed, wk_ref[...]).astype(BF)
    v_ref[0] = mm(normed, wv_ref[...]).astype(BF)


def project(x, sw, gain, wq, wk, wv):
    frames, depth, streams = x.shape
    width = wq.shape[0]
    local = wq.shape[1]
    whole = lambda shape: pl.BlockSpec(shape, lambda t: (0,) * len(shape))
    row = lambda w: pl.BlockSpec((1, streams, w), lambda t: (t, 0, 0))
    return pl.pallas_call(
        project_kernel,
        grid=(frames,),
        in_specs=[
            pl.BlockSpec((1, depth, streams), lambda t: (t, 0, 0)),
            whole(sw.shape),
            whole(gain.shape),
            whole(wq.shape),
            whole(wk.shape),
            whole(wv.shape),
        ],
        out_specs=[row(width), row(local), row(local), row(local)],
        out_shape=[jax.ShapeDtypeStruct((frames, streams, width), BF)]
        + [jax.ShapeDtypeStruct((frames, streams, local), BF)] * 3,
        compiler_params=pltpu.CompilerParams(vmem_limit_bytes=VMEM_LIMIT),
        cost_estimate=pl.CostEstimate(flops=2600000000, bytes_accessed=25000000, transcendentals=1000),
        name="project",
    )(x, sw, gain, wq, wk, wv)


def attend_kernel(
    has_ref, q_ref, kn_ref, vn_ref, kc_ref, vc_ref, kr_ref, vr_ref, pick_ref, bits_ref, stay_ref,
    colbias_ref, match_ref, ctx_ref, ko_ref, vo_ref, kall, vall,
):
    group = pl.program_id(0)
    local = q_ref.shape[2]
    slots = kr_ref.shape[1]
    span = pick_ref.shape[2] // slots
    kall[0:CACHE] = kc_ref[...]
    vall[0:CACHE] = vc_ref[...]

    @pl.when(has_ref[group] > 0)
    def _():
        stay = (stay_ref[...] > 0.5)[None]
        for first in range(0, CACHE, span):
            count = min(span, CACHE - first)
            pick = pick_ref[0, : count * GROUP, : count * slots]
            for rec, dest in ((kr_ref, kall), (vr_ref, vall)):
                rows = rec[first : first + count].reshape(count * slots, local)
                fetched = mm(pick, rows).astype(BF).reshape(count, GROUP, local)
                dest[first : first + count] = jnp.where(stay, dest[first : first + count], fetched)

    kall[CACHE:TOTAL] = kn_ref[...]
    vall[CACHE:TOTAL] = vn_ref[...]
    bias = match_ref[...] + colbias_ref[0]
    for h in range(local // HEAD):
        lanes = slice(h * HEAD, (h + 1) * HEAD)
        qh = q_ref[:, :, lanes].reshape(FRAMES * GROUP, HEAD)
        kh = kall[:, :, lanes].reshape(TOTAL * GROUP, HEAD)
        vh = vall[:, :, lanes].reshape(TOTAL * GROUP, HEAD)
        scores = lax.dot_general(qh, kh, (((1,), (1,)), ((), ())), preferred_element_type=F32)
        scores = scores * (1.0 / math.sqrt(HEAD)) + bias
        peak = jnp.max(scores, axis=-1, keepdims=True)
        expo = jnp.exp(scores - peak)
        weights = (expo * (1.0 / jnp.sum(expo, axis=-1, keepdims=True))).astype(BF)
        ctx_ref[0, :, lanes] = mm(weights, vh).astype(BF)
    masks = [bits_ref[b] > 0.5 for b in range(3)]
    step = 10
    for src, dst in ((kall, ko_ref), (vall, vo_ref)):
        for first in range(0, CACHE, step):
            dst[first : first + step] = shift_rows(src[first : first + step + FRAMES], masks)


def attend(has, q, kn, vn, kc, vc, kr, vr, pick, bits, stay, colbias, match):
    streams, local = q.shape[1:]
    groups = streams // GROUP
    slots = kr.shape[1]
    block = lambda n: pl.BlockSpec((n, GROUP, local), lambda g, *_: (0, g, 0))
    whole = lambda shape: pl.BlockSpec(shape, lambda g, *_: (0,) * len(shape))
    return pl.pallas_call(
        attend_kernel,
        grid_spec=pltpu.PrefetchScalarGridSpec(
            num_scalar_prefetch=1,
            grid=(groups,),
            in_specs=[
                block(FRAMES), block(FRAMES), block(FRAMES), block(CACHE), block(CACHE),
                whole(kr.shape), whole(vr.shape),
                pl.BlockSpec((1,) + pick.shape[1:], lambda g, *_: (g, 0, 0)),
                block(3),
                pl.BlockSpec((GROUP, local), lambda g, *_: (g, 0)),
                pl.BlockSpec((1, 1, TOTAL * GROUP), lambda g, *_: (g, 0, 0)),
                whole(match.shape),
            ],
            out_specs=[
                pl.BlockSpec((1, FRAMES * GROUP, local), lambda g, *_: (g, 0, 0)), block(CACHE), block(CACHE),
            ],
            scratch_shapes=[pltpu.VMEM((TOTAL, GROUP, local), BF)] * 2,
        ),
        out_shape=[
            jax.ShapeDtypeStruct((groups, FRAMES * GROUP, local), BF),
            jax.ShapeDtypeStruct((CACHE, streams, local), BF),
            jax.ShapeDtypeStruct((CACHE, streams, local), BF),
        ],
        compiler_params=pltpu.CompilerParams(vmem_limit_bytes=VMEM_LIMIT),
        cost_estimate=pl.CostEstimate(flops=1200000000, bytes_accessed=20000000, transcendentals=2500000),
        name="attend",
    )(has, q, kn, vn, kc, vc, kr, vr, pick, bits, stay, colbias, match)


def tail_kernel(
    parts, chunks, ctx_ref, in_ref, wo_ref, gain_ref, wv_ref, wg_ref, conv_ref, bits_ref, dk_ref, scale_ref,
    bias_ref, wc_ref, valid_ref, enc_ref, co_ref, ctx_all, act_all, middle_own, middle_now, conv_all,
    ctx_send, ctx_recv, act_send, act_recv,
):
    me = lax.axis_index("enc")
    local = ctx_ref.shape[2]
    width = in_ref.shape[2]
    rows = FRAMES * GROUP
    last = parts - 1
    right = lax.rem(me + 1, parts)
    left = lax.rem(me + parts - 1, parts)
    mesh_ids = pl.DeviceIdType.MESH

    barrier = pltpu.get_barrier_semaphore()

    @pl.when(me > 0)
    def _():
        pl.semaphore_signal(barrier, inc=1, device_id={"enc": left}, device_id_type=mesh_ids)

    @pl.when(me < last)
    def _():
        pl.semaphore_signal(barrier, inc=1, device_id={"enc": right}, device_id_type=mesh_ids)

    inner = (me > 0) & (me < last)

    @pl.when(inner)
    def _():
        pl.semaphore_wait(barrier, 2)

    @pl.when(jnp.logical_not(inner))
    def _():
        pl.semaphore_wait(barrier, 1)

    def hop(line, source, chunk, way):
        buffer, send, recv = line
        return pltpu.make_async_remote_copy(
            src_ref=buffer.at[source, chunk],
            dst_ref=buffer.at[source, chunk],
            send_sem=send.at[way, source, chunk],
            recv_sem=recv.at[source, chunk],
            device_id={"enc": (right, left)[way]},
            device_id_type=mesh_ids,
        )

    def send_own(line, chunk):
        @pl.when(me < last)
        def _():
            hop(line, me, chunk, 0).start()

        @pl.when(me > 0)
        def _():
            hop(line, me, chunk, 1).start()

    def pass_on(line, chunk, distance):
        @pl.when(me >= distance)
        def _():
            copy = hop(line, me - distance, chunk, 0)
            copy.wait_recv()

            @pl.when(me < last)
            def _():
                copy.start()

        @pl.when(me + distance <= last)
        def _():
            copy = hop(line, me + distance, chunk, 1)
            copy.wait_recv()

            @pl.when(me > 0)
            def _():
                copy.start()

    def sent(line, chunk):
        for source in range(parts):
            @pl.when((me >= source) & (me < last))
            def _():
                hop(line, source, chunk, 0).wait_send()

            @pl.when((me <= source) & (me > 0))
            def _():
                hop(line, source, chunk, 1).wait_send()

    def convolve(chunk):
        here = pl.ds(pl.multiple_of(chunk * GROUP, GROUP), GROUP)
        attended = jnp.zeros((rows, width), F32)
        for g in range(parts):
            share = mm(ctx_all[g, chunk], wo_ref[g * local : (g + 1) * local])
            attended = attended + share.astype(BF).astype(F32)
        middle = (in_ref[:, here, :].reshape(rows, width).astype(F32) + attended).astype(BF)
        middle_now[...] = middle
        middle_own[chunk] = middle_now[:, pl.ds(pl.multiple_of(me * local, local), local)]
        normed = layer_norm(middle.astype(F32), gain_ref[...]).astype(BF)
        gated = (mm(normed, wv_ref[...]) * jax.nn.sigmoid(mm(normed, wg_ref[...]))).astype(BF)
        conv_all[0:CONV_CACHE] = conv_ref[:, here, :]
        conv_all[CONV_CACHE:] = gated.reshape(FRAMES, GROUP, local)
        for t in range(FRAMES):
            total = jnp.zeros((GROUP, local), F32)
            for k in range(KERNEL):
                total = total + dk_ref[k : k + 1, :] * conv_all[t + k].astype(F32)
            shaped = total * scale_ref[...] + bias_ref[...]
            active = (shaped * jax.nn.sigmoid(shaped)).astype(BF)
            act_all[me, chunk, t * GROUP : (t + 1) * GROUP] = active
        masks = [bits_ref[b, here, :] > 0.5 for b in range(3)]
        co_ref[:, here, :] = shift_rows(conv_all[...], masks)

    def finish(chunk):
        here = pl.ds(pl.multiple_of(chunk * GROUP, GROUP), GROUP)
        total = jnp.zeros((rows, local), F32)
        for g in range(parts):
            share = mm(act_all[g, chunk], wc_ref[lax.rem(me + parts - g, parts)])
            total = total + share.astype(BF).astype(F32)
        total = (total + middle_own[chunk].astype(F32)).reshape(FRAMES, GROUP, local)
        valid = valid_ref[here, :]
        for t in range(FRAMES):
            enc_ref[t, here, :] = jnp.where(valid > t + 0.5, total[t], 0.0).astype(BF)

    ctx_all[me] = ctx_ref[...]
    ctx_line = (ctx_all, ctx_send, ctx_recv)
    act_line = (act_all, act_send, act_recv)

    def turn(step, carry):
        def at(lag, action):
            chunk = step - lag

            @pl.when((chunk >= 0) & (chunk < chunks))
            def _():
                action(chunk)

        def middle_part(chunk):
            pass_on(ctx_line, chunk, last)
            convolve(chunk)
            send_own(act_line, chunk)

        def end_part(chunk):
            pass_on(act_line, chunk, last)
            finish(chunk)

        at(0, lambda c: send_own(ctx_line, c))
        for d in range(1, last):
            at(d, lambda c, d=d: pass_on(ctx_line, c, d))
        at(last, middle_part)
        for d in range(1, last):
            at(last + d, lambda c, d=d: pass_on(act_line, c, d))
        at(2 * last, end_part)
        return carry

    lax.fori_loop(0, chunks + 2 * last, turn, 0)

    def drain(chunk, carry):
        sent(ctx_line, chunk)
        sent(act_line, chunk)
        return carry

    lax.fori_loop(0, chunks, drain, 0)


def tail(parts, ctx, inputs, wo, gain, wv, wg, conv, bits, dk, scale, bias, wc, valid_wide):
    chunks, rows, local = ctx.shape
    frames, streams, width = inputs.shape
    vmem = pl.BlockSpec(memory_space=pltpu.VMEM)
    return pl.pallas_call(
        functools.partial(tail_kernel, parts, chunks),
        in_specs=[vmem] * 13,
        out_specs=[vmem] * 2,
        out_shape=[
            jax.ShapeDtypeStruct((frames, streams, local), BF),
            jax.ShapeDtypeStruct((CONV_CACHE, streams, local), BF),
        ],
        scratch_shapes=[
            pltpu.VMEM((parts, chunks, rows, local), BF),
            pltpu.VMEM((parts, chunks, rows, local), BF),
            pltpu.VMEM((chunks, rows, local), BF),
            pltpu.VMEM((rows, width), BF),
            pltpu.VMEM((CONV_CACHE + frames, GROUP, local), BF),
            pltpu.SemaphoreType.DMA((2, parts, chunks)),
            pltpu.SemaphoreType.DMA((parts, chunks)),
            pltpu.SemaphoreType.DMA((2, parts, chunks)),
            pltpu.SemaphoreType.DMA((parts, chunks)),
        ],
        compiler_params=pltpu.CompilerParams(
            vmem_limit_bytes=VMEM_LIMIT, collective_id=0, has_side_effects=True
        ),
        cost_estimate=pl.CostEstimate(flops=4000000000, bytes_accessed=10000000, transcendentals=1000000),
        name="tail",
    )(ctx, inputs, wo, gain, wv, wg, conv, bits, dk, scale, bias, wc, valid_wide)


def on_device(
    spectra,
    sub_weight,
    sub_bias,
    key_cache,
    value_cache,
    conv_cache,
    new_slot,
    old_slot,
    valid_new,
    cache_fill,
    ln1_gain,
    w_query,
    w_key,
    w_value,
    w_attn_out,
    ln2_gain,
    w_glu_value,
    w_glu_gate,
    depth_kernel,
    norm_scale,
    norm_shift,
    w_conv_out,
):
    peer_count = lax.axis_size("front")
    own_index = lax.axis_index("front")
    streams = spectra.shape[0]
    local = w_query.shape[1]
    slots = peer_count * CAP
    mels = spectra.shape[2]

    def gather_shared(weight):
        share = weight.shape[0] // peer_count
        own = lax.dynamic_slice_in_dim(weight, own_index * share, share, 0)
        return lax.all_gather(own, ("enc", "front"), tiled=True)

    bias_rows = -sub_weight.shape[0] % (8 * peer_count) or 8 * peer_count
    bias_rows = jnp.broadcast_to(sub_bias[None], (bias_rows, local))
    sub_full = gather_shared(jnp.concatenate([sub_weight, bias_rows], axis=0))
    sub_full = sub_full.reshape(lax.axis_size("enc"), -1, local)
    attn_full = gather_shared(w_attn_out)
    parts = lax.axis_size("enc")
    member = lax.axis_index("enc")
    conv_cols = []
    for shift in range(parts):
        piece = lax.dynamic_slice_in_dim(w_conv_out, lax.rem(member + shift, parts) * local, local, 1)
        if shift:
            piece = lax.ppermute(piece, "enc", [(m, (m + shift) % parts) for m in range(parts)])
        conv_cols.append(piece)
    conv_cols = jnp.stack(conv_cols)

    leaving = send_slots(new_slot, own_index, peer_count, streams).astype(BF)
    arrival, staying = arrival_slots(old_slot, own_index, slots)
    arriving = (arrival[:, None] == jnp.arange(slots, dtype=jnp.int32)[None, :]).astype(BF)

    x = spectra.transpose(1, 2, 0).reshape(FRAMES * SUB * mels, streams)
    x_send = lax.dot_general(leaving, x, (((1,), (1,)), ((), ())), preferred_element_type=F32).astype(BF)
    x_recv = lax.all_to_all(x_send, "front", split_axis=0, concat_axis=0, tiled=True)
    x_moved = lax.dot_general(x_recv, arriving, (((0,), (1,)), ((), ())), preferred_element_type=F32).astype(BF)
    x_new = jnp.where(staying[None, :], x, x_moved).reshape(FRAMES, SUB * mels, streams)

    keys = key_cache.transpose(1, 0, 2)
    values = value_cache.transpose(1, 0, 2)
    conv = conv_cache.transpose(1, 0, 2)
    choose = lambda a: jnp.einsum("rs,jsc->rjc", leaving, a, preferred_element_type=F32).astype(BF)
    bundle = jnp.concatenate([choose(keys), choose(values), choose(conv)], axis=1)
    recv = lax.all_to_all(bundle, "front", split_axis=0, concat_axis=0, tiled=True)
    inputs, queries, key_new, value_new = project(
        x_new, sub_full, ln1_gain[None], w_query, w_key, w_value
    )
    recv, queries = lax.optimization_barrier((recv, queries))
    recv = recv.transpose(1, 0, 2)
    keys_recv, values_recv = recv[:CACHE], recv[CACHE : 2 * CACHE]
    conv_moved = jnp.einsum(
        "sr,jrc->jsc", arriving, recv[2 * CACHE :], preferred_element_type=F32
    ).astype(BF)
    conv_old = jnp.where(staying[None, :, None], conv, conv_moved)

    groups = streams // GROUP
    span = max(1, 256 // slots)
    wanted = jnp.tile(arrival.reshape(groups, GROUP), (1, span))
    spot = np.arange(span * slots, dtype=np.int32)
    block_of = np.arange(span * GROUP, dtype=np.int32) // GROUP
    slot_in = np.where(block_of[:, None] == (spot // slots)[None, :], (spot % slots)[None, :], -1)
    pick = (wanted[:, :, None] == slot_in.astype(np.int32)[None]).astype(BF)
    has = jnp.sum((~staying).astype(jnp.int32).reshape(groups, GROUP), axis=1)
    valid_wide = jnp.broadcast_to(valid_new.astype(F32)[:, None], (streams, local))
    bits = jnp.stack([(valid_new >> b) & 1 for b in range(3)]).astype(BF)
    bits = jnp.broadcast_to(bits[:, :, None], (3, streams, local))
    stay_wide = jnp.broadcast_to(staying.astype(BF)[:, None], (streams, local))
    col = np.arange(TOTAL * GROUP, dtype=np.int32)
    row = np.arange(FRAMES * GROUP, dtype=np.int32)
    least = jnp.tile((CACHE - cache_fill).reshape(groups, GROUP), (1, TOTAL))
    most = jnp.tile((CACHE + valid_new).reshape(groups, GROUP), (1, TOTAL))
    spread_col = (col // GROUP)[None, :]
    colbias = jnp.where((spread_col >= least) & (spread_col < most), 0.0, masked_score)
    colbias = colbias.astype(F32)[:, None, :]
    match = jnp.asarray(
        np.where((row % GROUP)[:, None] == (col % GROUP)[None, :], 0.0, masked_score).astype(np.float32)
    )

    context, key_out, value_out = attend(
        has, queries, key_new, value_new, keys, values, keys_recv, values_recv, pick, bits, stay_wide,
        colbias, match,
    )
    encoded, conv_out = tail(
        parts, context, inputs, attn_full, ln2_gain[None], w_glu_value, w_glu_gate, conv_old,
        bits, depth_kernel, norm_scale[None], norm_shift[None], conv_cols, valid_wide,
    )
    back = lambda a: a.transpose(1, 0, 2)
    return back(encoded), back(key_out), back(value_out), back(conv_out)


def solution(mesh):
    in_specs = (
        P("front", None, None),
        P(None, "enc"),
        P("enc"),
        P("front", None, "enc"),
        P("front", None, "enc"),
        P("front", None, "enc"),
        P("front"),
        P("front"),
        P("front"),
        P("front"),
        P(),
        P(None, "enc"),
        P(None, "enc"),
        P(None, "enc"),
        P("enc", None),
        P(),
        P(None, "enc"),
        P(None, "enc"),
        P(None, "enc"),
        P("enc"),
        P("enc"),
        P("enc", None),
    )
    out_specs = (P("front", None, "enc"),) * 4
    return jax.shard_map(
        on_device, mesh=mesh, in_specs=in_specs, out_specs=out_specs, check_vma=False
    )
```
